32 devices in a mesh: runs: 2 (over y), tiles: 16 (over z, x, core).
Axes of the slice: x: 2, y: 2, z: 4, core: 2. Of those that a mesh axis runs over, the one named last changes fastest.
Arguments:
- features: bfloat16 [32, 256, 2048], P(('runs', 'tiles')), parts along dimension 0, may hold values from -6 to 6
- conv_weight: bfloat16 [2, 2, 9, 256, 256], replicated, may hold values from -0.125 to 0.125
- proj_weight: bfloat16 [2, 256, 128], replicated, may hold values from -0.375 to 0.375
- back_weight: bfloat16 [2, 128, 256], replicated, may hold values from -0.5 to 0.5
- sea_fraction: float32 [16, 2048], P('tiles'), may hold values from 0 to 1
- halo_source: int32 [16, 2, 128], P('tiles'), may hold values from 0 to 256, as said below
- src_cells: int32 [16, 5, 4, 128], P('tiles'), may hold values from 0 to 2047
- dst_cells: int32 [16, 5, 4, 128], P('tiles'), may hold values from 0 to 2048, as said below
Outputs:
- updated: bfloat16 [32, 256, 2048], P(('runs', 'tiles')), parts along dimension 0
The draws below stay inside these ranges and needn't reach their ends.
There are 2 independent parts, one for each index of `runs`. The reference program is written for one: setup_inputs(seed, part) draws one part's arguments, and reference() takes and returns one part's arrays. A program takes and returns all parts, laid end to end along the dimension named above; an argument that names none is the same for every part. Nothing has to cross between parts.
Inputs may be any that keep to these rules, and one draw needn't show every extreme that they name: `halo_source`: the value 2 * 128 means a zero halo cell and occurs on the lower side of the ocean tile of local index 0; the atmosphere tiles at both ends of their arc and the last ocean tile read their own edge row on their outer side. `dst_cells`: entry 2048 marks an unused block; a block is used only if its source tile lies in the other component, and every tile uses all 4 blocks of offset 0.
All inputs are finite; a program needn't handle non-finite values.
Results may differ from the reference program's by a relative error of at most 0.0085.
Values may be sent and summed in bfloat16 or wider, within the bound.
A program may use at most 64 MiB of HBM per device.

```python
import jax
import jax.numpy as jnp
from jax import lax

C = 256
PROJ = 128
TH = 16
W = 128
BLOCK = 128
CAP = 4
REACH = 2
OFFSETS = 5
CELLS = 2048
TILE_COUNT = 16
HALF = 8


def draw_halo_source(key, part):
    tile = jnp.arange(TILE_COUNT, dtype=jnp.int32)[:, None, None]
    side = jnp.arange(2, dtype=jnp.int32)[None, :, None]
    column = jnp.arange(W, dtype=jnp.int32)[None, None, :]
    shift_amount = jax.random.randint(jax.random.fold_in(key, 11), (TILE_COUNT, 2, 1), 0, W)
    inner = (column + shift_amount) % W
    position = (tile + HALF // 2) % TILE_COUNT
    local = position % HALF
    ocean = position >= HALF
    polar = W + (column + W // 2) % W
    folded = W + (W - 1 - column)
    zeroed = jnp.zeros_like(inner) + 2 * W
    lower_end = (local == 0) & (side == 0)
    upper_end = (local == HALF - 1) & (side == 1)
    value = jnp.where(lower_end, jnp.where(ocean, zeroed, polar), jnp.where(upper_end, jnp.where(ocean, folded, polar), inner))
    return value.astype(jnp.int32)


def draw_dst_cells(key, part):
    tile = jnp.arange(TILE_COUNT, dtype=jnp.int32)[:, None, None, None]
    slot = jnp.arange(OFFSETS, dtype=jnp.int32)[None, :, None, None]
    entry = jnp.arange(CAP, dtype=jnp.int32)[None, None, :, None]
    position = (tile + HALF // 2) % TILE_COUNT
    local = position % HALF
    source_local = local - (slot - REACH)
    valid = (source_local >= 0) & (source_local < HALF)
    used_count = jax.random.randint(jax.random.fold_in(key, 21), (TILE_COUNT, OFFSETS, 1, 1), 1, CAP + 1)
    used_count = jnp.where(slot == REACH, CAP, used_count)
    used = valid & (entry < used_count)
    cell = jax.random.randint(jax.random.fold_in(key, 22), (TILE_COUNT, OFFSETS, CAP, BLOCK), 0, CELLS)
    return jnp.where(used, cell, CELLS).astype(jnp.int32)


def plant(array, rng, smallest, largest):
    index_at = [jax.random.randint(jax.random.fold_in(rng, axis), (), 0, length) for axis, length in enumerate(array.shape)]
    longest = array.shape.index(max(array.shape))
    next_to = index_at[:longest] + [(index_at[longest] + 1) % array.shape[longest]] + index_at[longest + 1:]
    return array.at[tuple(index_at)].set(smallest).at[tuple(next_to)].set(largest)


def levels(stream_key, dims, split, smallest, high):
    factor_of = 1.0
    for axis_at, blocks in split:
        heights = jax.random.uniform(jax.random.fold_in(jax.random.fold_in(stream_key, 6), axis_at), (blocks,), jnp.float32, smallest / len(split), high / len(split))
        factor_of = factor_of * jnp.repeat(jnp.exp(heights), dims[axis_at] // blocks).reshape((-1,) + (1,) * (len(dims) - 1 - axis_at))
    return factor_of


def noise(key, extent, spread, reach, shards=(), held_as=jnp.bfloat16):
    loudness = levels(key, extent, shards, -0.22, 0.18) if shards else 1.0
    entries = jax.random.normal(key, extent, jnp.float32) * spread * loudness
    return jnp.minimum(jnp.maximum(entries, -reach), reach).astype(held_as)


def setup_inputs(seed: int = 0, part: int = 0) -> dict:
    streams_of = jax.random.split(jax.random.key(seed), 9)
    part_splits = jax.random.split(jax.random.fold_in(streams_of[8], part), 9)
    return {
        "features": noise(part_splits[0], (TILE_COUNT, C, CELLS), 1.0, 6.0, ((0, 16),)),
        "conv_weight": noise(streams_of[1], (2, 2, 9, C, C), (9 * C) ** -0.5, 0.125),
        "proj_weight": noise(streams_of[2], (2, C, PROJ), C ** -0.5, 0.375),
        "back_weight": noise(streams_of[3], (2, PROJ, C), PROJ ** -0.5, 0.5),
        "sea_fraction": jnp.clip(1.0 * jax.random.uniform(streams_of[4], (TILE_COUNT, CELLS), jnp.float32) ** levels(streams_of[4], (TILE_COUNT, CELLS), ((0, 16),), -0.2, 0.2), 0.0, 1.0),
        "halo_source": draw_halo_source(jax.random.fold_in(streams_of[8], 71), part),
        "src_cells": plant(jax.random.randint(streams_of[6], (TILE_COUNT, OFFSETS, CAP, BLOCK), 0, CELLS), jax.random.fold_in(streams_of[6], 1), 0, CELLS - 1).astype(jnp.int32),
        "dst_cells": draw_dst_cells(jax.random.fold_in(streams_of[8], 71), part),
    }


def activate(values):
    return jax.nn.gelu(values.astype(jnp.float32), approximate=True).astype(jnp.bfloat16)


def convolve(kernel, padded):
    result = jnp.zeros((kernel.shape[2], TH, W), jnp.float32)
    for row_off in range(3):
        for col_off in range(3):
            shifted = jnp.roll(padded[:, row_off:row_off + TH, :], 1 - col_off, axis=2)
            result = result + jnp.einsum('io,irc->orc', kernel[row_off * 3 + col_off].astype(jnp.float32), shifted.astype(jnp.float32))
    return result


def residual_block(state, layer, conv_weight, component, wet_weight, halo_source):
    activated = activate(state).reshape(TILE_COUNT, C, TH, W)
    first_rows = activated[:, :, 0, :]
    last_rows = activated[:, :, TH - 1, :]
    from_below = jnp.roll(last_rows, 1, axis=0)
    from_above = jnp.roll(first_rows, -1, axis=0)
    zero_col = jnp.zeros((TILE_COUNT, C, 1), jnp.bfloat16)
    lower_src = jnp.concatenate([from_below, first_rows, zero_col], axis=2)
    upper_src = jnp.concatenate([from_above, last_rows, zero_col], axis=2)
    pick = jax.vmap(lambda source, index: jnp.take(source, index, axis=1))
    lower_row = pick(lower_src, halo_source[:, 0])
    upper_row = pick(upper_src, halo_source[:, 1])
    padded = jnp.concatenate([lower_row[:, :, None], activated, upper_row[:, :, None]], axis=2)

    def one_tile(inputs):
        pad_tile, comp_tile, state_tile, wet_tile = inputs
        kernel = conv_weight[comp_tile, layer]
        conv = convolve(kernel, pad_tile).reshape(C, CELLS)
        return (state_tile.astype(jnp.float32) + wet_tile[None, :] * conv).astype(jnp.bfloat16)

    return lax.map(one_tile, (padded, component, state, wet_weight))


def remap_add(state, component, proj_weight, back_weight, src_cells, dst_cells):
    def project(inputs):
        state_tile, comp_tile = inputs
        return jnp.einsum('cn,ck->nk', state_tile.astype(jnp.float32), proj_weight[comp_tile].astype(jnp.float32)).astype(jnp.bfloat16)

    projected = lax.map(project, (state, component))
    blocks = jax.vmap(lambda table, index: table[index])(projected, src_cells)
    incoming = jnp.stack([jnp.roll(blocks[:, slot], HALF + slot - REACH, axis=0) for slot in range(OFFSETS)], axis=1)

    def land(received, index):
        summed = jnp.zeros((CELLS, PROJ), jnp.float32)
        return summed.at[index.reshape(-1)].add(received.reshape(-1, PROJ).astype(jnp.float32), mode='drop')

    remapped = jax.vmap(land)(incoming, dst_cells).astype(jnp.bfloat16)

    def add_back(inputs):
        state_tile, remap_tile, comp_tile = inputs
        returned = jnp.einsum('nk,ko->on', remap_tile.astype(jnp.float32), back_weight[comp_tile].astype(jnp.float32))
        return (state_tile.astype(jnp.float32) + returned).astype(jnp.bfloat16)

    return lax.map(add_back, (state, remapped, component))


def reference(features, conv_weight, proj_weight, back_weight, sea_fraction, halo_source, src_cells, dst_cells):
    position = (jnp.arange(TILE_COUNT, dtype=jnp.int32) + HALF // 2) % TILE_COUNT
    component = (position >= HALF).astype(jnp.int32)
    wet_weight = jnp.where(component[:, None] == 1, sea_fraction, jnp.float32(1.0))
    state = residual_block(features, 0, conv_weight, component, wet_weight, halo_source)
    state = remap_add(state, component, proj_weight, back_weight, src_cells, dst_cells)
    state = residual_block(state, 1, conv_weight, component, wet_weight, halo_source)
    return state
```

```python
import functools

import jax
import jax.numpy as jnp
from jax import lax
from jax.experimental import pallas as pl
from jax.experimental.pallas import tpu as pltpu
from jax.sharding import PartitionSpec as P

F32 = jnp.float32
BF16 = jnp.bfloat16


def gelu(x):
    return jax.nn.gelu(x, approximate=True)


def spread(row, width):
    return jnp.broadcast_to(row, (width, row.shape[1])).T


def forecast_kernel(
    tiles,
    features,
    conv_weight,
    proj_weight,
    back_weight,
    sea_fraction,
    halo_source,
    src_cells,
    dst_cells,
    out,
    xs,
    st,
    pad,
    cw,
    pw,
    bw,
    sea,
    halo,
    src,
    dst,
    wet,
    srcb,
    hot_low,
    hot_up,
    edge,
    proj,
    outgoing,
    incoming,
    land,
    summed,
    result,
    in_sem,
    out_dma_sem,
    halo_send,
    halo_recv,
    block_send,
    block_recv,
):
    half = tiles // 2
    me = lax.axis_index("tiles")
    pos = lax.rem(me + half // 2, tiles)
    comp = pos // half
    local = lax.rem(pos, half)
    channels, cells = xs.shape
    row = halo.shape[1]
    rows = cells // row
    offsets = incoming.shape[0]
    per_slot = incoming.shape[1]
    reach = offsets // 2
    coupling = pw.shape[1]
    up = lax.rem(me + 1, tiles)
    down = lax.rem(me + tiles - 1, tiles)

    def local_copy(source, target, slot):
        return pltpu.make_async_copy(source, target, in_sem.at[slot])

    loads = [
        local_copy(features.at[0], xs, 0),
        local_copy(halo_source.at[0], halo, 1),
        local_copy(src_cells, src, 2),
        local_copy(dst_cells, dst, 3),
        local_copy(sea_fraction, sea, 4),
        local_copy(conv_weight.at[comp, 0], cw.at[0], 5),
        local_copy(proj_weight.at[comp], pw, 6),
        local_copy(back_weight.at[comp], bw, 7),
        local_copy(conv_weight.at[comp, 1], cw.at[1], 8),
    ]
    for load in loads:
        load.start()

    def partner(slot):
        return lax.rem(me + half + slot - reach + tiles, tiles)

    barrier = pltpu.get_barrier_semaphore()
    for other in [up, down] + [partner(s) for s in range(offsets)]:
        pl.semaphore_signal(
            barrier, inc=1, device_id={"tiles": other}, device_id_type=pl.DeviceIdType.MESH
        )

    def at(r):
        return pl.ds(pl.multiple_of(r * row, row), row)

    def put_activated(r, x):
        g = gelu(x)
        where = at(r + 1)
        pad[where, 0:channels] = pltpu.roll(g, 1, 0).astype(BF16)
        pad[where, channels : 2 * channels] = g.astype(BF16)
        pad[where, 2 * channels : 3 * channels] = pltpu.roll(g, row - 1, 0).astype(BF16)

    def halo_copies(block):
        mid = pl.ds(channels, channels)
        to_down = pltpu.make_async_remote_copy(
            src_ref=pad.at[pl.ds(row, row), mid],
            dst_ref=edge.at[block, 1, pl.ds(0, row)],
            send_sem=halo_send.at[block, 0],
            recv_sem=halo_recv.at[block, 1],
            device_id={"tiles": down},
            device_id_type=pl.DeviceIdType.MESH,
        )
        to_up = pltpu.make_async_remote_copy(
            src_ref=pad.at[pl.ds(rows * row, row), mid],
            dst_ref=edge.at[block, 0, pl.ds(0, row)],
            send_sem=halo_send.at[block, 1],
            recv_sem=halo_recv.at[block, 0],
            device_id={"tiles": up},
            device_id_type=pl.DeviceIdType.MESH,
        )
        return to_down, to_up

    def conv(block, first, count):
        span = count * row
        windows = [
            pad[pl.ds(pl.multiple_of((first + a) * row, row), span), :] for a in range(3)
        ]
        taps = cw[block].reshape(9 * channels, channels)
        return jnp.dot(
            jnp.concatenate(windows, axis=1), taps, preferred_element_type=F32
        )

    def updated(block, first, count):
        where = pl.ds(pl.multiple_of(first * row, row), count * row)
        w = wet[where, :]
        w = jnp.concatenate([w] * (channels // w.shape[1]), axis=1)
        return (st[where, :].astype(F32) + w * conv(block, first, count)).astype(BF16)

    def place_halo(block):
        for side, hot, target in ((0, hot_low, 0), (1, hot_up, rows + 1)):
            own = pad[pl.ds(row if side == 0 else rows * row, row), channels : 2 * channels]
            pair = jnp.concatenate([edge[block, side], own], axis=0)
            taken = jnp.dot(hot[...], pair, preferred_element_type=F32).astype(BF16)
            for b in range(3):
                pad[pl.ds(target * row, row), b * channels : (b + 1) * channels] = taken[
                    b * row : (b + 1) * row
                ]

    def load_row(r):
        x = xs[:, at(r)].astype(F32).T
        st[at(r), :] = x.astype(BF16)
        put_activated(r, x)

    loads[0].wait()
    load_row(0)
    load_row(rows - 1)
    pl.semaphore_wait(barrier, offsets + 2)
    for copy in halo_copies(0):
        copy.start()

    @pl.loop(1, rows - 1)
    def _(r):
        load_row(r)

    for load in loads[1:5]:
        load.wait()

    for side, hot in ((0, hot_low), (1, hot_up)):
        column = spread(halo[side : side + 1, :], row)
        column = jnp.concatenate([column, column], axis=1)
        lane = lax.broadcasted_iota(jnp.int32, column.shape, 1)
        one = jnp.where(column == lane, 1.0, 0.0).astype(F32)
        hot[0:row] = pltpu.roll(one, 1, 0).astype(BF16)
        hot[row : 2 * row] = one.astype(BF16)
        hot[2 * row : 3 * row] = pltpu.roll(one, row - 1, 0).astype(BF16)

    for r in range(rows):
        values = spread(sea[0:1, r * row : (r + 1) * row], row)
        wet[r * row : (r + 1) * row, :] = jnp.where(comp == 1, values, F32(1.0))

    for s in range(offsets):
        for e in range(per_slot // row):
            index = s * (per_slot // row) + e
            srcb[index * row : (index + 1) * row, :] = spread(src[0, s, e : e + 1, :], row)

    loads[5].wait()
    loads[6].wait()

    def block_zero(first, count):
        new = updated(0, first, count)
        where = pl.ds(pl.multiple_of(first * row, row), count * row)
        st[where, :] = new
        proj[where, :] = jnp.dot(new, pw[...], preferred_element_type=F32).astype(BF16)

    group = (rows - 2) // 2

    @pl.loop(0, 2)
    def _(g):
        block_zero(1 + g * group, group)

    for copy in halo_copies(0):
        copy.wait()
    place_halo(0)
    block_zero(0, 1)
    block_zero(rows - 1, 1)

    def block_copy(s):
        return pltpu.make_async_remote_copy(
            src_ref=outgoing.at[s],
            dst_ref=incoming.at[s],
            send_sem=block_send.at[s],
            recv_sem=block_recv.at[s],
            device_id={"tiles": partner(s)},
            device_id_type=pl.DeviceIdType.MESH,
        )

    def sends(s):
        there = local + s - reach
        return jnp.logical_and(there >= 0, there < half)

    def receives(s):
        there = local - s + reach
        return jnp.logical_and(there >= 0, there < half)

    order = sorted(range(offsets), key=lambda s: (abs(s - reach), s))

    for s in order:
        @pl.when(sends(s))
        def _(s=s):
            lane = lax.broadcasted_iota(jnp.int32, (per_slot, row), 1)
            cell = srcb[s * per_slot : (s + 1) * per_slot, :]
            hot = jnp.concatenate(
                [jnp.where(cell == lane + r * row, 1.0, 0.0).astype(BF16) for r in range(rows)],
                axis=1,
            )
            outgoing[s] = jnp.dot(hot, proj[...], preferred_element_type=F32).astype(BF16)
            block_copy(s).start()

    @pl.loop(0, rows)
    def _(r):
        cell = lax.broadcasted_iota(jnp.int32, (row, row), 0) + r * row
        for s in range(offsets):
            for e in range(per_slot // row):
                target = dst[0, s, e : e + 1, :]
                land[at(r), s * per_slot + e * row : s * per_slot + (e + 1) * row] = jnp.where(
                    target == cell, 1.0, 0.0
                ).astype(BF16)

    summed[...] = jnp.zeros_like(summed)
    loads[7].wait()
    loads[8].wait()

    chunk = 4 * row
    for s in order:
        @pl.when(receives(s))
        def _(s=s):
            block_copy(s).wait_recv()

            @pl.loop(0, cells // chunk)
            def _(c):
                where = pl.ds(pl.multiple_of(c * chunk, chunk), chunk)
                summed[where, :] += jnp.dot(
                    land[where, s * per_slot : (s + 1) * per_slot],
                    incoming[s],
                    preferred_element_type=F32,
                )

    def add_back(r):
        remapped = summed[at(r), :].astype(BF16)
        returned = jnp.dot(remapped, bw[...], preferred_element_type=F32)
        new = (st[at(r), :].astype(F32) + returned).astype(BF16)
        st[at(r), :] = new
        put_activated(r, new.astype(F32))

    add_back(0)
    add_back(rows - 1)
    for copy in halo_copies(1):
        copy.start()

    @pl.loop(1, rows - 1)
    def _(r):
        add_back(r)

    def block_one(first, count):
        new = updated(1, first, count).astype(F32)
        for i in range(count):
            result[:, at(first + i)] = new[i * row : (i + 1) * row].T.astype(BF16)

    def result_copy(first, count, slot):
        lanes = pl.ds(first * row, count * row)
        return pltpu.make_async_copy(
            result.at[:, lanes], out.at[0, :, lanes], out_dma_sem.at[slot]
        )

    @pl.loop(0, 2)
    def _(g):
        block_one(1 + g * group, group)

    middle = result_copy(1, rows - 2, 0)
    middle.start()
    for copy in halo_copies(1):
        copy.wait()
    place_halo(1)
    block_one(0, 1)
    low = result_copy(0, 1, 1)
    low.start()
    block_one(rows - 1, 1)
    high = result_copy(rows - 1, 1, 2)
    high.start()
    for s in order:
        @pl.when(sends(s))
        def _(s=s):
            block_copy(s).wait_send()
    middle.wait()
    low.wait()
    high.wait()


def on_device(
    features, conv_weight, proj_weight, back_weight, sea_fraction, halo_source, src_cells, dst_cells
):
    tiles = lax.axis_size("tiles")
    _, channels, cells = features.shape
    row = halo_source.shape[2]
    _, offsets, slots, block = src_cells.shape
    coupling = proj_weight.shape[2]
    per_slot = slots * block
    rows = cells // row
    taps = conv_weight.shape[2]
    flops = 4 * cells * taps * channels * channels + 4 * offsets * per_slot * cells * coupling
    return pl.pallas_call(
        functools.partial(forecast_kernel, tiles),
        out_shape=jax.ShapeDtypeStruct(features.shape, BF16),
        in_specs=[pl.BlockSpec(memory_space=pl.ANY)] * 8,
        out_specs=pl.BlockSpec(memory_space=pl.ANY),
        scratch_shapes=[
            pltpu.VMEM((channels, cells), BF16),
            pltpu.VMEM((cells, channels), BF16),
            pltpu.VMEM(((rows + 2) * row, 3 * channels), BF16),
            pltpu.VMEM((2, taps, channels, channels), BF16),
            pltpu.VMEM((channels, coupling), BF16),
            pltpu.VMEM((coupling, channels), BF16),
            pltpu.VMEM((1, cells), F32),
            pltpu.VMEM((2, row), jnp.int32),
            pltpu.VMEM(src_cells.shape, jnp.int32),
            pltpu.VMEM(dst_cells.shape, jnp.int32),
            pltpu.VMEM((cells, row), F32),
            pltpu.VMEM((offsets * per_slot, row), jnp.int32),
            pltpu.VMEM((3 * row, 2 * row), BF16),
            pltpu.VMEM((3 * row, 2 * row), BF16),
            pltpu.VMEM((2, 2, row, channels), BF16),
            pltpu.VMEM((cells, coupling), BF16),
            pltpu.VMEM((offsets, per_slot, coupling), BF16),
            pltpu.VMEM((offsets, per_slot, coupling), BF16),
            pltpu.VMEM((cells, offsets * per_slot), BF16),
            pltpu.VMEM((cells, coupling), F32),
            pltpu.VMEM((channels, cells), BF16),
            pltpu.SemaphoreType.DMA((9,)),
            pltpu.SemaphoreType.DMA((3,)),
            pltpu.SemaphoreType.DMA((2, 2)),
            pltpu.SemaphoreType.DMA((2, 2)),
            pltpu.SemaphoreType.DMA((offsets,)),
            pltpu.SemaphoreType.DMA((offsets,)),
        ],
        compiler_params=pltpu.CompilerParams(
            collective_id=0, has_side_effects=True, vmem_limit_bytes=56 * 1024 * 1024
        ),
        cost_estimate=pl.CostEstimate(
            flops=flops, bytes_accessed=8 * channels * cells, transcendentals=2 * channels * cells
        ),
    )(
        features,
        conv_weight,
        proj_weight,
        back_weight,
        sea_fraction,
        halo_source,
        src_cells,
        dst_cells,
    )


def solution(mesh):
    placed = (
        P(("runs", "tiles"), None, None),
        P(),
        P(),
        P(),
        P("tiles", None),
        P("tiles", None, None),
        P("tiles", None, None, None),
        P("tiles", None, None, None),
    )
    return jax.shard_map(
        on_device,
        mesh=mesh,
        in_specs=placed,
        out_specs=P(("runs", "tiles"), None, None),
        check_vma=False,
    )
```

```python
import functools

import jax
import jax.numpy as jnp
from jax import lax
from jax.experimental import pallas as pl
from jax.experimental.pallas import tpu as pltpu
from jax.sharding import PartitionSpec as P

F32 = jnp.float32
BF16 = jnp.bfloat16


def gelu(x):
    return jax.nn.gelu(x, approximate=True)


def spread(row, width):
    return jnp.broadcast_to(row, (width, row.shape[1])).T


def forecast_kernel(
    tiles,
    features,
    conv_weight,
    proj_weight,
    back_weight,
    sea_fraction,
    halo_source,
    src_cells,
    dst_cells,
    out,
    xs,
    st,
    pad,
    cw,
    pw,
    bw,
    sea,
    halo,
    src,
    dst,
    wet,
    srcb,
    hot_low,
    hot_up,
    edge,
    proj,
    outgoing,
    incoming,
    land,
    summed,
    in_sem,
    halo_send,
    halo_recv,
    block_send,
    block_recv,
):
    half = tiles // 2
    me = lax.axis_index("tiles")
    pos = lax.rem(me + half // 2, tiles)
    comp = pos // half
    local = lax.rem(pos, half)
    channels, cells = xs.shape
    row = halo.shape[1]
    rows = cells // row
    offsets = incoming.shape[0]
    per_slot = incoming.shape[1]
    reach = offsets // 2
    coupling = pw.shape[1]
    up = lax.rem(me + 1, tiles)
    down = lax.rem(me + tiles - 1, tiles)

    def local_copy(source, target, slot):
        return pltpu.make_async_copy(source, target, in_sem.at[slot])

    loads = [
        local_copy(halo_source.at[0], halo, 1),
        local_copy(src_cells, src, 2),
        local_copy(sea_fraction, sea, 4),
        local_copy(features.at[0], xs, 0),
        local_copy(conv_weight.at[comp, 0], cw.at[0], 5),
        local_copy(proj_weight.at[comp], pw, 6),
        local_copy(dst_cells, dst, 3),
        local_copy(back_weight.at[comp], bw, 7),
        local_copy(conv_weight.at[comp, 1], cw.at[1], 8),
    ]
    for load in loads:
        load.start()

    def partner(slot):
        return lax.rem(me + half + slot - reach + tiles, tiles)

    barrier = pltpu.get_barrier_semaphore()
    for other in [up, down] + [partner(s) for s in range(offsets)]:
        pl.semaphore_signal(
            barrier, inc=1, device_id={"tiles": other}, device_id_type=pl.DeviceIdType.MESH
        )

    def at(r):
        return pl.ds(pl.multiple_of(r * row, row), row)

    def put_activated(r, x):
        g = gelu(x)
        where = at(r + 1)
        pad[where, 0:channels] = pltpu.roll(g, 1, 0).astype(BF16)
        pad[where, channels : 2 * channels] = g.astype(BF16)
        pad[where, 2 * channels : 3 * channels] = pltpu.roll(g, row - 1, 0).astype(BF16)

    def halo_copies(block):
        mid = pl.ds(channels, channels)
        to_down = pltpu.make_async_remote_copy(
            src_ref=pad.at[pl.ds(row, row), mid],
            dst_ref=edge.at[block, 1, pl.ds(0, row)],
            send_sem=halo_send.at[block, 0],
            recv_sem=halo_recv.at[block, 1],
            device_id={"tiles": down},
            device_id_type=pl.DeviceIdType.MESH,
        )
        to_up = pltpu.make_async_remote_copy(
            src_ref=pad.at[pl.ds(rows * row, row), mid],
            dst_ref=edge.at[block, 0, pl.ds(0, row)],
            send_sem=halo_send.at[block, 1],
            recv_sem=halo_recv.at[block, 0],
            device_id={"tiles": up},
            device_id_type=pl.DeviceIdType.MESH,
        )
        return to_down, to_up

    def conv(block, first, count):
        span = count * row
        windows = [
            pad[pl.ds(pl.multiple_of((first + a) * row, row), span), :] for a in range(3)
        ]
        taps = cw[block].reshape(9 * channels, channels)
        return jnp.dot(
            jnp.concatenate(windows, axis=1), taps, preferred_element_type=F32
        )

    def updated(block, first, count):
        where = pl.ds(pl.multiple_of(first * row, row), count * row)
        w = wet[where, :]
        w = jnp.concatenate([w] * (channels // w.shape[1]), axis=1)
        return (st[where, :].astype(F32) + w * conv(block, first, count)).astype(BF16)

    def place_halo(block):
        for side, hot, target in ((0, hot_low, 0), (1, hot_up, rows + 1)):
            own = pad[pl.ds(row if side == 0 else rows * row, row), channels : 2 * channels]
            pair = jnp.concatenate([edge[block, side], own], axis=0)
            taken = jnp.dot(hot[...], pair, preferred_element_type=F32).astype(BF16)
            for b in range(3):
                pad[pl.ds(target * row, row), b * channels : (b + 1) * channels] = taken[
                    b * row : (b + 1) * row
                ]

    def load_row(r):
        x = xs[:, at(r)].astype(F32).T
        st[at(r), :] = x.astype(BF16)
        put_activated(r, x)

    for load in loads[0:3]:
        load.wait()

    for side, hot in ((0, hot_low), (1, hot_up)):
        column = spread(halo[side : side + 1, :], row)
        column = jnp.concatenate([column, column], axis=1)
        lane = lax.broadcasted_iota(jnp.int32, column.shape, 1)
        one = jnp.where(column == lane, 1.0, 0.0).astype(F32)
        hot[0:row] = pltpu.roll(one, 1, 0).astype(BF16)
        hot[row : 2 * row] = one.astype(BF16)
        hot[2 * row : 3 * row] = pltpu.roll(one, row - 1, 0).astype(BF16)

    @pl.loop(0, rows)
    def _(r):
        values = spread(sea[0:1, at(r)], row)
        wet[at(r), :] = jnp.where(comp == 1, values, F32(1.0))

    slots = per_slot // row

    @pl.loop(0, offsets)
    def _(s):
        for e in range(slots):
            srcb[at(s * slots + e), :] = spread(src[0, s, e : e + 1, :], row)

    loads[3].wait()

    @pl.loop(0, 2)
    def _(g):
        load_row(g * (rows - 1))

    pl.semaphore_wait(barrier, offsets + 2)
    for copy in halo_copies(0):
        copy.start()

    @pl.loop(1, rows - 1)
    def _(r):
        load_row(r)

    loads[4].wait()
    loads[5].wait()

    def block_zero(first, count):
        new = updated(0, first, count)
        where = pl.ds(pl.multiple_of(first * row, row), count * row)
        st[where, :] = new
        proj[where, :] = jnp.dot(new, pw[...], preferred_element_type=F32).astype(BF16)

    group = 2

    @pl.loop(0, (rows - 2) // group)
    def _(g):
        block_zero(1 + g * group, group)

    for copy in halo_copies(0):
        copy.wait()
    place_halo(0)

    @pl.loop(0, 2)
    def _(g):
        block_zero(g * (rows - 1), 1)

    def block_copy(s):
        return pltpu.make_async_remote_copy(
            src_ref=outgoing.at[s],
            dst_ref=incoming.at[s],
            send_sem=block_send.at[s],
            recv_sem=block_recv.at[s],
            device_id={"tiles": partner(s)},
            device_id_type=pl.DeviceIdType.MESH,
        )

    def sends(s):
        there = local + s - reach
        return jnp.logical_and(there >= 0, there < half)

    def receives(s):
        there = local - s + reach
        return jnp.logical_and(there >= 0, there < half)

    def slot_at(k):
        return reach + (1 - 2 * lax.rem(k, 2)) * ((k + 1) // 2)

    @pl.loop(0, offsets)
    def _(k):
        s = slot_at(k)

        @pl.when(sends(s))
        def _():
            lane = lax.broadcasted_iota(jnp.int32, (per_slot, row), 1)
            cell = srcb[pl.ds(pl.multiple_of(s * per_slot, per_slot), per_slot), :]
            hot = jnp.concatenate(
                [jnp.where(cell == lane + r * row, 1.0, 0.0).astype(BF16) for r in range(rows)],
                axis=1,
            )
            outgoing[s] = jnp.dot(hot, proj[...], preferred_element_type=F32).astype(BF16)
            block_copy(s).start()

    loads[6].wait()

    @pl.loop(0, rows)
    def _(r):
        cell = lax.broadcasted_iota(jnp.int32, (row, row), 0) + r * row
        for s in range(offsets):
            for e in range(slots):
                target = dst[0, s, e : e + 1, :]
                land[at(r), s * per_slot + e * row : s * per_slot + (e + 1) * row] = jnp.where(
                    target == cell, 1.0, 0.0
                ).astype(BF16)

    summed[...] = jnp.zeros_like(summed)
    loads[7].wait()
    loads[8].wait()

    chunk = 4 * row
    @pl.loop(0, offsets)
    def _(k):
        s = slot_at(k)

        @pl.when(receives(s))
        def _():
            block_copy(s).wait_recv()

            @pl.loop(0, cells // chunk)
            def _(c):
                where = pl.ds(pl.multiple_of(c * chunk, chunk), chunk)
                summed[where, :] += jnp.dot(
                    land[where, pl.ds(pl.multiple_of(s * per_slot, per_slot), per_slot)],
                    incoming[s],
                    preferred_element_type=F32,
                )

    def add_back(r):
        remapped = summed[at(r), :].astype(BF16)
        returned = jnp.dot(remapped, bw[...], preferred_element_type=F32)
        new = (st[at(r), :].astype(F32) + returned).astype(BF16)
        st[at(r), :] = new
        put_activated(r, new.astype(F32))

    @pl.loop(0, 2)
    def _(g):
        add_back(g * (rows - 1))

    for copy in halo_copies(1):
        copy.start()

    @pl.loop(1, rows - 1)
    def _(r):
        add_back(r)

    def block_one(first, count):
        new = updated(1, first, count).astype(F32)
        for i in range(count):
            out[0, :, at(first + i)] = new[i * row : (i + 1) * row].T.astype(BF16)

    @pl.loop(0, (rows - 2) // group)
    def _(g):
        block_one(1 + g * group, group)

    for copy in halo_copies(1):
        copy.wait()
    place_halo(1)

    @pl.loop(0, 2)
    def _(g):
        block_one(g * (rows - 1), 1)

    @pl.loop(0, offsets)
    def _(s):
        @pl.when(sends(s))
        def _():
            block_copy(s).wait_send()


def on_device(
    features, conv_weight, proj_weight, back_weight, sea_fraction, halo_source, src_cells, dst_cells
):
    tiles = lax.axis_size("tiles")
    _, channels, cells = features.shape
    row = halo_source.shape[2]
    _, offsets, slots, block = src_cells.shape
    coupling = proj_weight.shape[2]
    per_slot = slots * block
    rows = cells // row
    taps = conv_weight.shape[2]
    flops = 4 * cells * taps * channels * channels + 4 * offsets * per_slot * cells * coupling
    return pl.pallas_call(
        functools.partial(forecast_kernel, tiles),
        out_shape=jax.ShapeDtypeStruct(features.shape, BF16),
        in_specs=[pl.BlockSpec(memory_space=pltpu.HBM)] * 8,
        out_specs=pl.BlockSpec(memory_space=pltpu.VMEM),
        scratch_shapes=[
            pltpu.VMEM((channels, cells), BF16),
            pltpu.VMEM((cells, channels), BF16),
            pltpu.VMEM(((rows + 2) * row, 3 * channels), BF16),
            pltpu.VMEM((2, taps, channels, channels), BF16),
            pltpu.VMEM((channels, coupling), BF16),
            pltpu.VMEM((coupling, channels), BF16),
            pltpu.VMEM((1, cells), F32),
            pltpu.VMEM((2, row), jnp.int32),
            pltpu.VMEM(src_cells.shape, jnp.int32),
            pltpu.VMEM(dst_cells.shape, jnp.int32),
            pltpu.VMEM((cells, row), F32),
            pltpu.VMEM((offsets * per_slot, row), jnp.int32),
            pltpu.VMEM((3 * row, 2 * row), BF16),
            pltpu.VMEM((3 * row, 2 * row), BF16),
            pltpu.VMEM((2, 2, row, channels), BF16),
            pltpu.VMEM((cells, coupling), BF16),
            pltpu.VMEM((offsets, per_slot, coupling), BF16),
            pltpu.VMEM((offsets, per_slot, coupling), BF16),
            pltpu.VMEM((cells, offsets * per_slot), BF16),
            pltpu.VMEM((cells, coupling), F32),
            pltpu.SemaphoreType.DMA((9,)),
            pltpu.SemaphoreType.DMA((2, 2)),
            pltpu.SemaphoreType.DMA((2, 2)),
            pltpu.SemaphoreType.DMA((offsets,)),
            pltpu.SemaphoreType.DMA((offsets,)),
        ],
        compiler_params=pltpu.CompilerParams(
            collective_id=0, has_side_effects=True, vmem_limit_bytes=40 * 1024 * 1024
        ),
        cost_estimate=pl.CostEstimate(
            flops=flops, bytes_accessed=8 * channels * cells, transcendentals=2 * channels * cells
        ),
    )(
        *(
            pltpu.with_memory_space_constraint(value, pltpu.HBM)
            for value in (
                features,
                conv_weight,
                proj_weight,
                back_weight,
                sea_fraction,
                halo_source,
                src_cells,
                dst_cells,
            )
        )
    )


def solution(mesh):
    placed = (
        P(("runs", "tiles"), None, None),
        P(),
        P(),
        P(),
        P("tiles", None),
        P("tiles", None, None),
        P("tiles", None, None, None),
        P("tiles", None, None, None),
    )
    return jax.shard_map(
        on_device,
        mesh=mesh,
        in_specs=placed,
        out_specs=P(("runs", "tiles"), None, None),
        check_vma=False,
    )
```

```python
import functools

import jax
import jax.numpy as jnp
from jax import lax
from jax.experimental import pallas as pl
from jax.experimental.pallas import tpu as pltpu
from jax.sharding import PartitionSpec as P

F32 = jnp.float32
BF16 = jnp.bfloat16


def gelu(x):
    return jax.nn.gelu(x, approximate=True)


def spread(row, width):
    return jnp.broadcast_to(row, (width, row.shape[1])).T


def forecast_kernel(
    tiles,
    features,
    conv_weight,
    proj_weight,
    back_weight,
    sea_fraction,
    halo_source,
    src_cells,
    dst_cells,
    out,
    xs,
    st,
    pad,
    cw,
    pw,
    bw,
    sea,
    halo,
    src,
    dst,
    wet,
    srcb,
    hot_low,
    hot_up,
    edge,
    proj,
    outgoing,
    incoming,
    land,
    summed,
    in_sem,
    halo_send,
    halo_recv,
    block_send,
    block_recv,
):
    half = tiles // 2
    me = lax.axis_index("tiles")
    pos = lax.rem(me + half // 2, tiles)
    comp = pos // half
    local = lax.rem(pos, half)
    channels, cells = xs.shape
    row = halo.shape[1]
    rows = cells // row
    offsets = incoming.shape[0]
    per_slot = incoming.shape[1]
    reach = offsets // 2
    coupling = pw.shape[1]
    up = lax.rem(me + 1, tiles)
    down = lax.rem(me + tiles - 1, tiles)

    def local_copy(source, target, slot):
        return pltpu.make_async_copy(source, target, in_sem.at[slot])

    loads = [
        local_copy(halo_source.at[0], halo, 1),
        local_copy(src_cells, src, 2),
        local_copy(sea_fraction, sea, 4),
        local_copy(features.at[0], xs, 0),
        local_copy(conv_weight.at[comp, 0], cw.at[0], 5),
        local_copy(proj_weight.at[comp], pw, 6),
        local_copy(dst_cells, dst, 3),
        local_copy(back_weight.at[comp], bw, 7),
        local_copy(conv_weight.at[comp, 1], cw.at[1], 8),
    ]
    for load in loads:
        load.start()

    def partner(slot):
        return lax.rem(me + half + slot - reach + tiles, tiles)

    barrier = pltpu.get_barrier_semaphore()
    for other in [up, down] + [partner(s) for s in range(offsets)]:
        pl.semaphore_signal(
            barrier, inc=1, device_id={"tiles": other}, device_id_type=pl.DeviceIdType.MESH
        )

    def at(r):
        return pl.ds(pl.multiple_of(r * row, row), row)

    def put_activated(r, x):
        g = gelu(x)
        where = at(r + 1)
        pad[where, 0:channels] = pltpu.roll(g, 1, 0).astype(BF16)
        pad[where, channels : 2 * channels] = g.astype(BF16)
        pad[where, 2 * channels : 3 * channels] = pltpu.roll(g, row - 1, 0).astype(BF16)

    def halo_copies(block):
        mid = pl.ds(channels, channels)
        to_down = pltpu.make_async_remote_copy(
            src_ref=pad.at[pl.ds(row, row), mid],
            dst_ref=edge.at[block, 1, pl.ds(0, row)],
            send_sem=halo_send.at[block, 0],
            recv_sem=halo_recv.at[block, 1],
            device_id={"tiles": down},
            device_id_type=pl.DeviceIdType.MESH,
        )
        to_up = pltpu.make_async_remote_copy(
            src_ref=pad.at[pl.ds(rows * row, row), mid],
            dst_ref=edge.at[block, 0, pl.ds(0, row)],
            send_sem=halo_send.at[block, 1],
            recv_sem=halo_recv.at[block, 0],
            device_id={"tiles": up},
            device_id_type=pl.DeviceIdType.MESH,
        )
        return to_down, to_up

    def conv(block, pieces):
        windows = [
            jnp.concatenate(
                [pad[first * row + a * row : (first + count + a) * row, :] for a in range(3)],
                axis=1,
            )
            for first, count in pieces
        ]
        taps = cw[block].reshape(9 * channels, channels)
        return jnp.dot(
            jnp.concatenate(windows, axis=0), taps, preferred_element_type=F32
        )

    def span(ref, pieces):
        return jnp.concatenate(
            [ref[first * row : (first + count) * row, :] for first, count in pieces], axis=0
        )

    def updated(block, pieces):
        w = span(wet, pieces)
        w = jnp.concatenate([w] * (channels // w.shape[1]), axis=1)
        return (span(st, pieces).astype(F32) + w * conv(block, pieces)).astype(BF16)

    inner = [(1, rows - 2)]
    rim = [(0, 1), (rows - 1, 1)]

    def place_halo(block):
        for side, hot, target in ((0, hot_low, 0), (1, hot_up, rows + 1)):
            own = pad[pl.ds(row if side == 0 else rows * row, row), channels : 2 * channels]
            pair = jnp.concatenate([edge[block, side], own], axis=0)
            taken = jnp.dot(hot[...], pair, preferred_element_type=F32).astype(BF16)
            for b in range(3):
                pad[pl.ds(target * row, row), b * channels : (b + 1) * channels] = taken[
                    b * row : (b + 1) * row
                ]

    def load_row(r):
        x = xs[:, at(r)].astype(F32).T
        st[at(r), :] = x.astype(BF16)
        put_activated(r, x)

    for load in loads[0:3]:
        load.wait()

    for side, hot in ((0, hot_low), (1, hot_up)):
        column = spread(halo[side : side + 1, :], row)
        column = jnp.concatenate([column, column], axis=1)
        lane = lax.broadcasted_iota(jnp.int32, column.shape, 1)
        one = jnp.where(column == lane, 1.0, 0.0).astype(F32)
        hot[0:row] = pltpu.roll(one, 1, 0).astype(BF16)
        hot[row : 2 * row] = one.astype(BF16)
        hot[2 * row : 3 * row] = pltpu.roll(one, row - 1, 0).astype(BF16)

    for r in range(rows):
        values = spread(sea[0:1, r * row : (r + 1) * row], row)
        wet[r * row : (r + 1) * row, :] = jnp.where(comp == 1, values, F32(1.0))

    slots = per_slot // row

    for s in range(offsets):
        for e in range(slots):
            i = s * slots + e
            srcb[i * row : (i + 1) * row, :] = spread(src[0, s, e : e + 1, :], row)

    loads[3].wait()

    @pl.loop(0, rows // 2)
    def _(g):
        load_row(2 * g)
        load_row(2 * g + 1)

    pl.semaphore_wait(barrier, offsets + 2)
    for copy in halo_copies(0):
        copy.start()

    loads[4].wait()
    loads[5].wait()

    def block_zero(pieces):
        new = updated(0, pieces)
        sent = jnp.dot(new, pw[...], preferred_element_type=F32).astype(BF16)
        done = 0
        for first, count in pieces:
            where = slice(first * row, (first + count) * row)
            part = slice(done * row, (done + count) * row)
            st[where, :] = new[part]
            proj[where, :] = sent[part]
            done += count

    block_zero(inner)
    for copy in halo_copies(0):
        copy.wait()
    place_halo(0)
    block_zero(rim)

    def block_copy(s):
        return pltpu.make_async_remote_copy(
            src_ref=outgoing.at[s],
            dst_ref=incoming.at[s],
            send_sem=block_send.at[s],
            recv_sem=block_recv.at[s],
            device_id={"tiles": partner(s)},
            device_id_type=pl.DeviceIdType.MESH,
        )

    def sends(s):
        there = local + s - reach
        return jnp.logical_and(there >= 0, there < half)

    def receives(s):
        there = local - s + reach
        return jnp.logical_and(there >= 0, there < half)

    def slot_at(k):
        return reach + (1 - 2 * lax.rem(k, 2)) * ((k + 1) // 2)

    @pl.loop(0, offsets)
    def _(k):
        s = slot_at(k)

        @pl.when(sends(s))
        def _():
            lane = lax.broadcasted_iota(jnp.int32, (per_slot, row), 1)
            cell = srcb[pl.ds(pl.multiple_of(s * per_slot, per_slot), per_slot), :]
            hot = jnp.concatenate(
                [jnp.where(cell == lane + r * row, 1.0, 0.0).astype(BF16) for r in range(rows)],
                axis=1,
            )
            outgoing[s] = jnp.dot(hot, proj[...], preferred_element_type=F32).astype(BF16)
            block_copy(s).start()

    loads[6].wait()

    @pl.loop(0, rows)
    def _(r):
        cell = lax.broadcasted_iota(jnp.int32, (row, row), 0) + r * row
        for s in range(offsets):
            for e in range(slots):
                target = dst[0, s, e : e + 1, :]
                land[at(r), s * per_slot + e * row : s * per_slot + (e + 1) * row] = jnp.where(
                    target == cell, 1.0, 0.0
                ).astype(BF16)

    summed[...] = jnp.zeros_like(summed)
    loads[7].wait()
    loads[8].wait()

    chunk = 8 * row
    @pl.loop(0, offsets)
    def _(k):
        s = slot_at(k)

        @pl.when(receives(s))
        def _():
            block_copy(s).wait_recv()

            @pl.loop(0, cells // chunk)
            def _(c):
                where = pl.ds(pl.multiple_of(c * chunk, chunk), chunk)
                summed[where, :] += jnp.dot(
                    land[where, pl.ds(pl.multiple_of(s * per_slot, per_slot), per_slot)],
                    incoming[s],
                    preferred_element_type=F32,
                )

    def add_back(first, count):
        where = pl.ds(pl.multiple_of(first * row, row), count * row)
        remapped = summed[where, :].astype(BF16)
        returned = jnp.dot(remapped, bw[...], preferred_element_type=F32)
        new = (st[where, :].astype(F32) + returned).astype(BF16)
        st[where, :] = new
        for i in range(count):
            put_activated(first + i, new[i * row : (i + 1) * row].astype(F32))

    @pl.loop(0, 2)
    def _(g):
        add_back(g * (rows - 1), 1)

    for copy in halo_copies(1):
        copy.start()

    @pl.loop(0, 2)
    def _(g):
        add_back(1 + g * ((rows - 2) // 2), (rows - 2) // 2)

    def block_one(pieces):
        new = updated(1, pieces).astype(F32)
        done = 0
        for first, count in pieces:
            for i in range(first, first + count):
                out[0, :, i * row : (i + 1) * row] = (
                    new[done * row : (done + 1) * row].T.astype(BF16)
                )
                done += 1

    block_one(inner)
    for copy in halo_copies(1):
        copy.wait()
    place_halo(1)
    block_one(rim)

    @pl.loop(0, offsets)
    def _(s):
        @pl.when(sends(s))
        def _():
            block_copy(s).wait_send()


def on_device(
    features, conv_weight, proj_weight, back_weight, sea_fraction, halo_source, src_cells, dst_cells
):
    tiles = lax.axis_size("tiles")
    _, channels, cells = features.shape
    row = halo_source.shape[2]
    _, offsets, slots, block = src_cells.shape
    coupling = proj_weight.shape[2]
    per_slot = slots * block
    rows = cells // row
    taps = conv_weight.shape[2]
    flops = 4 * cells * taps * channels * channels + 4 * offsets * per_slot * cells * coupling
    return pl.pallas_call(
        functools.partial(forecast_kernel, tiles),
        out_shape=jax.ShapeDtypeStruct(features.shape, BF16),
        in_specs=[pl.BlockSpec(memory_space=pltpu.HBM)] * 8,
        out_specs=pl.BlockSpec(memory_space=pltpu.VMEM),
        scratch_shapes=[
            pltpu.VMEM((channels, cells), BF16),
            pltpu.VMEM((cells, channels), BF16),
            pltpu.VMEM(((rows + 2) * row, 3 * channels), BF16),
            pltpu.VMEM((2, taps, channels, channels), BF16),
            pltpu.VMEM((channels, coupling), BF16),
            pltpu.VMEM((coupling, channels), BF16),
            pltpu.VMEM((1, cells), F32),
            pltpu.VMEM((2, row), jnp.int32),
            pltpu.VMEM(src_cells.shape, jnp.int32),
            pltpu.VMEM(dst_cells.shape, jnp.int32),
            pltpu.VMEM((cells, row), F32),
            pltpu.VMEM((offsets * per_slot, row), jnp.int32),
            pltpu.VMEM((3 * row, 2 * row), BF16),
            pltpu.VMEM((3 * row, 2 * row), BF16),
            pltpu.VMEM((2, 2, row, channels), BF16),
            pltpu.VMEM((cells, coupling), BF16),
            pltpu.VMEM((offsets, per_slot, coupling), BF16),
            pltpu.VMEM((offsets, per_slot, coupling), BF16),
            pltpu.VMEM((cells, offsets * per_slot), BF16),
            pltpu.VMEM((cells, coupling), F32),
            pltpu.SemaphoreType.DMA((9,)),
            pltpu.SemaphoreType.DMA((2, 2)),
            pltpu.SemaphoreType.DMA((2, 2)),
            pltpu.SemaphoreType.DMA((offsets,)),
            pltpu.SemaphoreType.DMA((offsets,)),
        ],
        compiler_params=pltpu.CompilerParams(
            collective_id=0, has_side_effects=True, vmem_limit_bytes=40 * 1024 * 1024
        ),
        cost_estimate=pl.CostEstimate(
            flops=flops, bytes_accessed=8 * channels * cells, transcendentals=2 * channels * cells
        ),
    )(
        *(
            pltpu.with_memory_space_constraint(value, pltpu.HBM)
            for value in (
                features,
                conv_weight,
                proj_weight,
                back_weight,
                sea_fraction,
                halo_source,
                src_cells,
                dst_cells,
            )
        )
    )


def solution(mesh):
    placed = (
        P(("runs", "tiles"), None, None),
        P(),
        P(),
        P(),
        P("tiles", None),
        P("tiles", None, None),
        P("tiles", None, None, None),
        P("tiles", None, None, None),
    )
    return jax.shard_map(
        on_device,
        mesh=mesh,
        in_specs=placed,
        out_specs=P(("runs", "tiles"), None, None),
        check_vma=False,
    )
```

```python
import functools

import jax
import jax.numpy as jnp
from jax import lax
from jax.experimental import pallas as pl
from jax.experimental.pallas import tpu as pltpu
from jax.sharding import PartitionSpec as P

F32 = jnp.float32
BF16 = jnp.bfloat16


def gelu(x):
    return jax.nn.gelu(x, approximate=True)


def spread(row, width):
    return jnp.broadcast_to(row, (width, row.shape[1])).T


def forecast_kernel(
    tiles,
    features,
    conv_weight,
    proj_weight,
    back_weight,
    sea_fraction,
    halo_source,
    src_cells,
    dst_cells,
    out,
    xs,
    st,
    pad,
    cw,
    pw,
    bw,
    sea,
    halo,
    src,
    dst,
    wet,
    srcb,
    hot_low,
    hot_up,
    edge,
    proj,
    outgoing,
    incoming,
    land,
    summed,
    in_sem,
    feature_sem,
    halo_send,
    halo_recv,
    block_send,
    block_recv,
):
    half = tiles // 2
    me = lax.axis_index("tiles")
    pos = lax.rem(me + half // 2, tiles)
    comp = pos // half
    local = lax.rem(pos, half)
    channels, cells = xs.shape
    row = halo.shape[1]
    rows = cells // row
    offsets = incoming.shape[0]
    per_slot = incoming.shape[1]
    reach = offsets // 2
    coupling = pw.shape[1]
    up = lax.rem(me + 1, tiles)
    down = lax.rem(me + tiles - 1, tiles)

    def local_copy(source, target, slot):
        return pltpu.make_async_copy(source, target, in_sem.at[slot])

    loads = [
        local_copy(halo_source.at[0], halo, 1),
        local_copy(src_cells, src, 2),
        local_copy(sea_fraction, sea, 4),
        local_copy(conv_weight.at[comp, 0], cw.at[0], 5),
        local_copy(proj_weight.at[comp], pw, 6),
        local_copy(dst_cells, dst, 3),
        local_copy(back_weight.at[comp], bw, 7),
        local_copy(conv_weight.at[comp, 1], cw.at[1], 8),
    ]
    pieces_in = 4
    quarter = rows // pieces_in

    def piece_load(g):
        lanes = pl.ds(pl.multiple_of(g * quarter * row, quarter * row), quarter * row)
        return pltpu.make_async_copy(
            features.at[0, :, lanes], xs.at[:, lanes], feature_sem.at[g]
        )

    for load in loads[:3]:
        load.start()
    for g in range(pieces_in):
        piece_load(g).start()
    for load in loads[3:]:
        load.start()

    def partner(slot):
        return lax.rem(me + half + slot - reach + tiles, tiles)

    barrier = pltpu.get_barrier_semaphore()
    for other in [up, down] + [partner(s) for s in range(offsets)]:
        pl.semaphore_signal(
            barrier, inc=1, device_id={"tiles": other}, device_id_type=pl.DeviceIdType.MESH
        )

    def at(r):
        return pl.ds(pl.multiple_of(r * row, row), row)

    def put_activated(r, x):
        g = gelu(x)
        where = at(r + 1)
        pad[where, 0:channels] = pltpu.roll(g, 1, 0).astype(BF16)
        pad[where, channels : 2 * channels] = g.astype(BF16)
        pad[where, 2 * channels : 3 * channels] = pltpu.roll(g, row - 1, 0).astype(BF16)

    def halo_copies(block):
        mid = pl.ds(channels, channels)
        to_down = pltpu.make_async_remote_copy(
            src_ref=pad.at[pl.ds(row, row), mid],
            dst_ref=edge.at[block, 1, pl.ds(0, row)],
            send_sem=halo_send.at[block, 0],
            recv_sem=halo_recv.at[block, 1],
            device_id={"tiles": down},
            device_id_type=pl.DeviceIdType.MESH,
        )
        to_up = pltpu.make_async_remote_copy(
            src_ref=pad.at[pl.ds(rows * row, row), mid],
            dst_ref=edge.at[block, 0, pl.ds(0, row)],
            send_sem=halo_send.at[block, 1],
            recv_sem=halo_recv.at[block, 0],
            device_id={"tiles": up},
            device_id_type=pl.DeviceIdType.MESH,
        )
        return to_down, to_up

    def conv(block, pieces):
        windows = [
            jnp.concatenate(
                [pad[first * row + a * row : (first + count + a) * row, :] for a in range(3)],
                axis=1,
            )
            for first, count in pieces
        ]
        taps = cw[block].reshape(9 * channels, channels)
        return jnp.dot(
            jnp.concatenate(windows, axis=0), taps, preferred_element_type=F32
        )

    def span(ref, pieces):
        return jnp.concatenate(
            [ref[first * row : (first + count) * row, :] for first, count in pieces], axis=0
        )

    def updated(block, pieces):
        w = span(wet, pieces)
        w = jnp.concatenate([w] * (channels // w.shape[1]), axis=1)
        return (span(st, pieces).astype(F32) + w * conv(block, pieces)).astype(BF16)

    inner = [(1, rows - 2)]
    rim = [(0, 1), (rows - 1, 1)]

    def place_halo(block):
        for side, hot, target in ((0, hot_low, 0), (1, hot_up, rows + 1)):
            own = pad[pl.ds(row if side == 0 else rows * row, row), channels : 2 * channels]
            pair = jnp.concatenate([edge[block, side], own], axis=0)
            taken = jnp.dot(hot[...], pair, preferred_element_type=F32).astype(BF16)
            for b in range(3):
                pad[pl.ds(target * row, row), b * channels : (b + 1) * channels] = taken[
                    b * row : (b + 1) * row
                ]

    def load_row(r):
        x = xs[:, at(r)].astype(F32).T
        st[at(r), :] = x.astype(BF16)
        put_activated(r, x)

    for load in loads[0:3]:
        load.wait()

    for side, hot in ((0, hot_low), (1, hot_up)):
        column = spread(halo[side : side + 1, :], row)
        column = jnp.concatenate([column, column], axis=1)
        lane = lax.broadcasted_iota(jnp.int32, column.shape, 1)
        one = jnp.where(column == lane, 1.0, 0.0).astype(F32)
        hot[0:row] = pltpu.roll(one, 1, 0).astype(BF16)
        hot[row : 2 * row] = one.astype(BF16)
        hot[2 * row : 3 * row] = pltpu.roll(one, row - 1, 0).astype(BF16)

    for r in range(rows):
        values = spread(sea[0:1, r * row : (r + 1) * row], row)
        wet[r * row : (r + 1) * row, :] = jnp.where(comp == 1, values, F32(1.0))

    slots = per_slot // row

    for s in range(offsets):
        for e in range(slots):
            i = s * slots + e
            srcb[i * row : (i + 1) * row, :] = spread(src[0, s, e : e + 1, :], row)

    @pl.loop(0, pieces_in)
    def _(g):
        piece_load(g).wait()
        for i in range(quarter):
            load_row(quarter * g + i)

    pl.semaphore_wait(barrier, offsets + 2)
    for copy in halo_copies(0):
        copy.start()

    loads[3].wait()
    loads[4].wait()

    def block_zero(pieces):
        new = updated(0, pieces)
        sent = jnp.dot(new, pw[...], preferred_element_type=F32).astype(BF16)
        done = 0
        for first, count in pieces:
            where = slice(first * row, (first + count) * row)
            part = slice(done * row, (done + count) * row)
            st[where, :] = new[part]
            proj[where, :] = sent[part]
            done += count

    block_zero(inner)
    for copy in halo_copies(0):
        copy.wait()
    place_halo(0)
    block_zero(rim)

    def block_copy(s):
        return pltpu.make_async_remote_copy(
            src_ref=outgoing.at[s],
            dst_ref=incoming.at[s],
            send_sem=block_send.at[s],
            recv_sem=block_recv.at[s],
            device_id={"tiles": partner(s)},
            device_id_type=pl.DeviceIdType.MESH,
        )

    def sends(s):
        there = local + s - reach
        return jnp.logical_and(there >= 0, there < half)

    def receives(s):
        there = local - s + reach
        return jnp.logical_and(there >= 0, there < half)

    def slot_at(k):
        return reach + (1 - 2 * lax.rem(k, 2)) * ((k + 1) // 2)

    loads[5].wait()

    def land_slot(s):
        @pl.loop(0, rows // 4)
        def _(q):
            for i in range(4):
                r = 4 * q + i
                cell = lax.broadcasted_iota(jnp.int32, (row, row), 0) + r * row
                hot = [
                    jnp.where(dst[0, s, e : e + 1, :] == cell, 1.0, 0.0).astype(BF16)
                    for e in range(slots)
                ]
                land[at(r), pl.ds(pl.multiple_of(s * per_slot, per_slot), per_slot)] = (
                    jnp.concatenate(hot, axis=1)
                )

    in_flight = 2

    @pl.loop(0, offsets)
    def _(k):
        s = slot_at(k)

        @pl.when(sends(s))
        def _():
            lane = lax.broadcasted_iota(jnp.int32, (per_slot, row), 1)
            cell = srcb[pl.ds(pl.multiple_of(s * per_slot, per_slot), per_slot), :]
            hot = jnp.concatenate(
                [jnp.where(cell == lane + r * row, 1.0, 0.0).astype(BF16) for r in range(rows)],
                axis=1,
            )
            outgoing[s] = jnp.dot(hot, proj[...], preferred_element_type=F32).astype(BF16)

        before = slot_at(lax.max(k - in_flight, 0))

        @pl.when(jnp.logical_and(k >= in_flight, sends(before)))
        def _():
            block_copy(before).wait_send()

        @pl.when(sends(s))
        def _():
            block_copy(s).start()

        land_slot(s)

    summed[...] = jnp.zeros_like(summed)
    loads[6].wait()
    loads[7].wait()

    chunk = 8 * row
    @pl.loop(0, offsets)
    def _(k):
        s = slot_at(k)

        @pl.when(receives(s))
        def _():
            block_copy(s).wait_recv()

            @pl.loop(0, cells // chunk)
            def _(c):
                where = pl.ds(pl.multiple_of(c * chunk, chunk), chunk)
                summed[where, :] += jnp.dot(
                    land[where, pl.ds(pl.multiple_of(s * per_slot, per_slot), per_slot)],
                    incoming[s],
                    preferred_element_type=F32,
                )

    def add_back(first, count):
        where = pl.ds(pl.multiple_of(first * row, row), count * row)
        remapped = summed[where, :].astype(BF16)
        returned = jnp.dot(remapped, bw[...], preferred_element_type=F32)
        new = (st[where, :].astype(F32) + returned).astype(BF16)
        st[where, :] = new
        for i in range(count):
            put_activated(first + i, new[i * row : (i + 1) * row].astype(F32))

    @pl.loop(0, 2)
    def _(g):
        add_back(g * (rows - 1), 1)

    for copy in halo_copies(1):
        copy.start()

    @pl.loop(0, 2)
    def _(g):
        add_back(1 + g * ((rows - 2) // 2), (rows - 2) // 2)

    def block_one(pieces):
        new = updated(1, pieces).astype(F32)
        done = 0
        for first, count in pieces:
            for i in range(first, first + count):
                out[0, :, i * row : (i + 1) * row] = (
                    new[done * row : (done + 1) * row].T.astype(BF16)
                )
                done += 1

    block_one(inner)
    for copy in halo_copies(1):
        copy.wait()
    place_halo(1)
    block_one(rim)

    @pl.loop(offsets - in_flight, offsets)
    def _(k):
        s = slot_at(k)

        @pl.when(sends(s))
        def _():
            block_copy(s).wait_send()


def on_device(
    features, conv_weight, proj_weight, back_weight, sea_fraction, halo_source, src_cells, dst_cells
):
    tiles = lax.axis_size("tiles")
    _, channels, cells = features.shape
    row = halo_source.shape[2]
    _, offsets, slots, block = src_cells.shape
    coupling = proj_weight.shape[2]
    per_slot = slots * block
    rows = cells // row
    taps = conv_weight.shape[2]
    flops = 4 * cells * taps * channels * channels + 4 * offsets * per_slot * cells * coupling
    return pl.pallas_call(
        functools.partial(forecast_kernel, tiles),
        out_shape=jax.ShapeDtypeStruct(features.shape, BF16),
        in_specs=[pl.BlockSpec(memory_space=pltpu.HBM)] * 8,
        out_specs=pl.BlockSpec(memory_space=pltpu.VMEM),
        scratch_shapes=[
            pltpu.VMEM((channels, cells), BF16),
            pltpu.VMEM((cells, channels), BF16),
            pltpu.VMEM(((rows + 2) * row, 3 * channels), BF16),
            pltpu.VMEM((2, taps, channels, channels), BF16),
            pltpu.VMEM((channels, coupling), BF16),
            pltpu.VMEM((coupling, channels), BF16),
            pltpu.VMEM((1, cells), F32),
            pltpu.VMEM((2, row), jnp.int32),
            pltpu.VMEM(src_cells.shape, jnp.int32),
            pltpu.VMEM(dst_cells.shape, jnp.int32),
            pltpu.VMEM((cells, row), F32),
            pltpu.VMEM((offsets * per_slot, row), jnp.int32),
            pltpu.VMEM((3 * row, 2 * row), BF16),
            pltpu.VMEM((3 * row, 2 * row), BF16),
            pltpu.VMEM((2, 2, row, channels), BF16),
            pltpu.VMEM((cells, coupling), BF16),
            pltpu.VMEM((offsets, per_slot, coupling), BF16),
            pltpu.VMEM((offsets, per_slot, coupling), BF16),
            pltpu.VMEM((cells, offsets * per_slot), BF16),
            pltpu.VMEM((cells, coupling), F32),
            pltpu.SemaphoreType.DMA((9,)),
            pltpu.SemaphoreType.DMA((4,)),
            pltpu.SemaphoreType.DMA((2, 2)),
            pltpu.SemaphoreType.DMA((2, 2)),
            pltpu.SemaphoreType.DMA((offsets,)),
            pltpu.SemaphoreType.DMA((offsets,)),
        ],
        compiler_params=pltpu.CompilerParams(
            collective_id=0, has_side_effects=True, vmem_limit_bytes=40 * 1024 * 1024
        ),
        cost_estimate=pl.CostEstimate(
            flops=flops, bytes_accessed=8 * channels * cells, transcendentals=2 * channels * cells
        ),
    )(
        *(
            pltpu.with_memory_space_constraint(value, pltpu.HBM)
            for value in (
                features,
                conv_weight,
                proj_weight,
                back_weight,
                sea_fraction,
                halo_source,
                src_cells,
                dst_cells,
            )
        )
    )


def solution(mesh):
    placed = (
        P(("runs", "tiles"), None, None),
        P(),
        P(),
        P(),
        P("tiles", None),
        P("tiles", None, None),
        P("tiles", None, None, None),
        P("tiles", None, None, None),
    )
    return jax.shard_map(
        on_device,
        mesh=mesh,
        in_specs=placed,
        out_specs=P(("runs", "tiles"), None, None),
        check_vma=False,
    )
```
